256 devices in a mesh: row: 8 (over y, z_lo), col: 4 (over z_hi), layer: 8 (over x, core).
Axes of the slice: x: 4, y: 4, z: 8 (z_hi: 4, z_lo: 2; z = z_hi * 2 + z_lo), core: 2. Of those that a mesh axis runs over, the one named last changes fastest.
Arguments:
- density: bfloat16 [512, 8, 128, 128], P(('row', 'col')), may hold values from -1.1953125 to 1.1953125
- tile_cols: int32 [512, 8], replicated, may hold values from 0 to 511, as said below
- out_cols: int32 [512, 8, 4], P(('row', 'col')), may hold values from 0 to 511, as said below
Outputs:
- purified: bfloat16 [512, 8, 4, 128, 128], P(('row', 'col'), 'layer')
The draws below stay inside these ranges and needn't reach their ends.
Inputs may be any that keep to these rules, and one draw needn't show every extreme that they name: Column set l holds the block columns c with (c // 2) % 8 == l; tile_cols[i, l] lies in column set l, so a block row has exactly one tile in each column set. For each i and l, the 4 block columns out_cols[i, l, :] are distinct and lie in column set l.
All inputs are finite; a program needn't handle non-finite values.
Results may differ from the reference program's by a relative error of at most 0.0044.
Values may be sent and summed in bfloat16 or wider, within the bound.
No kernel may reach another device: no remote copies, remote signals or barrier semaphores. Data moves between devices by JAX's collectives and lax.ppermute only.
A program may use at most 128 MiB of HBM per device.

```python
import jax
import jax.numpy as jnp
from jax import lax

BS = 128
GROUP_ROWS = 16
KQ = 4
LAYERS = 8
GROUPS = 32
SUB_ROWS = 2
NB = 512


def settle(candidate, earlier):
    shifts = [(candidate + j * GROUP_ROWS) % NB for j in range(KQ)]
    stacked = jnp.stack(shifts, axis=-1)
    if earlier:
        unused = jnp.stack([jnp.all(jnp.stack([shifted != before for before in earlier], axis=0), axis=0) for shifted in shifts], axis=-1)
    else:
        unused = jnp.ones(stacked.shape, dtype=bool)
    chosen_shift = jnp.argmax(unused.astype(jnp.int32), axis=-1)
    return jnp.take_along_axis(stacked, chosen_shift[..., None], axis=-1)[..., 0]


def pattern(key):
    groups_drawn = jax.random.randint(jax.random.fold_in(key, 101), (NB, LAYERS), 0, GROUPS)
    within = jax.random.randint(jax.random.fold_in(key, 202), (NB, LAYERS), 0, SUB_ROWS)
    set_ids = jnp.arange(LAYERS, dtype=jnp.int32)[None, :]
    tile_cols = (groups_drawn * GROUP_ROWS + set_ids * SUB_ROWS + within).astype(jnp.int32)
    set_grid = jnp.arange(LAYERS, dtype=jnp.int32)[None, :, None]
    slot_draw = jax.random.randint(jax.random.fold_in(key, 303), (NB, LAYERS * 2), 0, LAYERS)
    through = jnp.take_along_axis(tile_cols, slot_draw, axis=1).reshape(NB, LAYERS, 2)
    reach_one = tile_cols[through, set_grid]
    slot_zero = settle(reach_one[:, :, 0], [])
    slot_one = settle(reach_one[:, :, 1], [slot_zero])
    base = jnp.stack([slot_zero, slot_one], axis=-1).reshape(NB, LAYERS * 2)
    via_draw = jax.random.randint(jax.random.fold_in(key, 404), (NB, LAYERS * 2), 0, LAYERS * 2)
    through_two = jnp.take_along_axis(base, via_draw, axis=1).reshape(NB, LAYERS, 2)
    reach_two = tile_cols[through_two, set_grid]
    slot_two = settle(reach_two[:, :, 0], [slot_zero, slot_one])
    slot_three = settle(reach_two[:, :, 1], [slot_zero, slot_one, slot_two])
    out_cols = jnp.stack([slot_zero, slot_one, slot_two, slot_three], axis=-1).astype(jnp.int32)
    return (tile_cols, out_cols)


def draw_tile_cols(key, part):
    return pattern(key)[0]


def draw_out_cols(key, part):
    return pattern(key)[1]


def steps_of(key, dims, split, low, top_value):
    factor_of = 1.0
    for axis_at, parts in split:
        heights = jax.random.uniform(jax.random.fold_in(jax.random.fold_in(key, 6), axis_at), (parts,), jnp.float32, low / len(split), top_value / len(split))
        factor_of = factor_of * jnp.repeat(jnp.exp(heights), dims[axis_at] // parts).reshape((-1,) + (1,) * (len(dims) - 1 - axis_at))
    return factor_of


def gaussian(stream_key, dims, width, most, cuts=(), kind=jnp.bfloat16):
    entries = jax.random.normal(stream_key, dims, jnp.float32) * width
    if len(cuts) > 0:
        entries = steps_of(stream_key, dims, cuts, -0.22, 0.18) * entries
    return jnp.clip(entries, min=-most, max=most).astype(kind)


def setup_inputs(seed: int = 0) -> dict:
    streams_of = jax.random.split(jax.random.key(seed), 4)
    density = gaussian(streams_of[0], (NB, LAYERS, BS, BS), 0.2, 1.1953125, ((0, 32),))
    tile_cols = draw_tile_cols(jax.random.fold_in(streams_of[3], 71), 0)
    out_cols = draw_out_cols(jax.random.fold_in(streams_of[3], 71), 0)
    return {"density": density, "tile_cols": tile_cols, "out_cols": out_cols}


def filtered_product(left_tiles, index_tiles, column, colset, wanted):
    step_rows = 32

    def row_block(first_row):
        left_part = lax.dynamic_slice_in_dim(left_tiles, first_row, step_rows, 0).astype(jnp.float32)
        index_part = lax.dynamic_slice_in_dim(index_tiles, first_row, step_rows, 0)
        wanted_part = lax.dynamic_slice_in_dim(wanted, first_row, step_rows, 0)
        b_tiles = jnp.take(column, index_part, axis=0).astype(jnp.float32)
        products = jnp.einsum("imab,imbc->imac", left_part, b_tiles, precision=lax.Precision.HIGHEST)
        matches = (jnp.take(colset, index_part, axis=0)[:, :, None] == wanted_part[:, None, :]).astype(jnp.float32)
        return jnp.einsum("imq,imac->iqac", matches, products, precision=lax.Precision.HIGHEST)

    starts = jnp.arange(left_tiles.shape[0] // step_rows, dtype=jnp.int32) * step_rows
    blocks = lax.map(row_block, starts)
    return blocks.reshape((left_tiles.shape[0],) + blocks.shape[2:])


def reference(density, tile_cols, out_cols):
    layer_ids = jnp.arange(LAYERS, dtype=jnp.int32)

    def square_set(layer_id):
        column = lax.dynamic_index_in_dim(density, layer_id, 1, keepdims=False)
        colset = lax.dynamic_index_in_dim(tile_cols, layer_id, 1, keepdims=False)
        wanted = lax.dynamic_index_in_dim(out_cols, layer_id, 1, keepdims=False)
        return filtered_product(density, tile_cols, column, colset, wanted)

    square = jnp.moveaxis(lax.map(square_set, layer_ids), 0, 1)
    square_low = square.astype(jnp.bfloat16).reshape(NB, LAYERS * KQ, BS, BS)
    cube_index = out_cols.reshape(NB, LAYERS * KQ)

    def purify_set(layer_id):
        column = lax.dynamic_index_in_dim(density, layer_id, 1, keepdims=False)
        colset = lax.dynamic_index_in_dim(tile_cols, layer_id, 1, keepdims=False)
        wanted = lax.dynamic_index_in_dim(out_cols, layer_id, 1, keepdims=False)
        cube = filtered_product(square_low, cube_index, column, colset, wanted)
        own_square = lax.dynamic_index_in_dim(square, layer_id, 1, keepdims=False)
        return (3.0 * own_square - 2.0 * cube).astype(jnp.bfloat16)

    return jnp.moveaxis(lax.map(purify_set, layer_ids), 0, 1)
```

```python
import jax
import jax.numpy as jnp
from jax import lax
from jax.experimental import pallas as pl
from jax.experimental.pallas import tpu as pltpu
from jax.sharding import Mesh
from jax.sharding import PartitionSpec as P

BATCH = 16
GROUP = 4
FIRST = 64
VMEM_LIMIT = 48 * 1024 * 1024


def square_kernel(jobs, count, left, right, square, square_low, left_buf, right_buf, total, left_sem, right_sem):
    outs = square.shape[0]
    batches = (count[0] + BATCH - 1) // BATCH
    total[...] = jnp.zeros_like(total)

    def start(batch):
        slot = lax.rem(batch, 2)
        for j in range(BATCH):
            word = jobs[batch * BATCH + j]
            pltpu.make_async_copy(left.at[(word >> 7) & 127], left_buf.at[slot, j], left_sem.at[slot]).start()
            pltpu.make_async_copy(right.at[word >> 14], right_buf.at[slot, j], right_sem.at[slot]).start()

    @pl.when(batches > 0)
    def _():
        start(0)

    def body(batch, carry):
        slot = lax.rem(batch, 2)

        @pl.when(batch + 1 < batches)
        def _():
            start(batch + 1)

        pltpu.make_async_copy(left_buf.at[slot], left_buf.at[slot], left_sem.at[slot]).wait()
        pltpu.make_async_copy(right_buf.at[slot], right_buf.at[slot], right_sem.at[slot]).wait()
        for first in range(0, BATCH, GROUP):
            products = [
                lax.dot_general(
                    right_buf[slot, j], left_buf[slot, j], (((1,), (1,)), ((), ())), preferred_element_type=jnp.float32
                )
                for j in range(first, first + GROUP)
            ]
            for j in range(GROUP):
                target = jobs[batch * BATCH + first + j] & 127
                total[target] += products[j]
        return carry

    lax.fori_loop(0, batches, body, 0)
    square[...] = total[:outs]
    square_low[...] = total[:outs].astype(jnp.bfloat16)


def square_part(jobs, count, left, right):
    part = right.shape[1]
    return pl.pallas_call(
        square_kernel,
        out_shape=(
            jax.ShapeDtypeStruct((64, part, 128), jnp.float32),
            jax.ShapeDtypeStruct((64, part, 128), jnp.bfloat16),
        ),
        in_specs=[
            pl.BlockSpec(memory_space=pltpu.SMEM),
            pl.BlockSpec(memory_space=pltpu.SMEM),
            pl.BlockSpec(memory_space=pl.ANY),
            pl.BlockSpec(memory_space=pl.ANY),
        ],
        out_specs=(pl.BlockSpec(memory_space=pltpu.VMEM), pl.BlockSpec(memory_space=pltpu.VMEM)),
        scratch_shapes=[
            pltpu.VMEM((2, BATCH, 128, 128), jnp.bfloat16),
            pltpu.VMEM((2, BATCH, part, 128), jnp.bfloat16),
            pltpu.VMEM((65, part, 128), jnp.float32),
            pltpu.SemaphoreType.DMA((2,)),
            pltpu.SemaphoreType.DMA((2,)),
        ],
        compiler_params=pltpu.CompilerParams(vmem_limit_bytes=VMEM_LIMIT),
        name="square_part",
    )(jobs, count, left, right)


def cube_kernel(*refs):
    jobs, count, right_a, right_b, square_a, square_b = refs[:6]
    pieces_a, pieces_b = refs[6:16], refs[16:26]
    out, right_buf, left_buf, total, right_sem, left_sem = refs[26:]
    first_part = square_a.shape[1]
    rest = 128 - first_part
    batches = (count[0] + BATCH - 1) // BATCH
    total[...] = jnp.zeros_like(total)

    def start(batch):
        slot = lax.rem(batch, 2)
        for j in range(BATCH):
            word = jobs[batch * BATCH + j]
            place = word >> 17
            piece = (word >> 13) & 15
            at = (word >> 7) & 63
            pltpu.make_async_copy(
                right_a.at[place], right_buf.at[slot, j, pl.ds(0, first_part)], right_sem.at[slot]
            ).start()
            pltpu.make_async_copy(
                right_b.at[place], right_buf.at[slot, j, pl.ds(first_part, rest)], right_sem.at[slot]
            ).start()
            for p in range(10):

                @pl.when(piece == p)
                def _(p=p, j=j, at=at):
                    pltpu.make_async_copy(
                        pieces_a[p].at[at], left_buf.at[slot, j, pl.ds(0, first_part)], left_sem.at[slot]
                    ).start()
                    pltpu.make_async_copy(
                        pieces_b[p].at[at], left_buf.at[slot, j, pl.ds(first_part, rest)], left_sem.at[slot]
                    ).start()

    @pl.when(batches > 0)
    def _():
        start(0)

    def body(batch, carry):
        slot = lax.rem(batch, 2)

        @pl.when(batch + 1 < batches)
        def _():
            start(batch + 1)

        pltpu.make_async_copy(right_buf.at[slot], right_buf.at[slot], right_sem.at[slot]).wait()
        pltpu.make_async_copy(left_buf.at[slot], left_buf.at[slot], left_sem.at[slot]).wait()
        for first in range(0, BATCH, GROUP):
            products = [
                jnp.dot(right_buf[slot, j], left_buf[slot, j], preferred_element_type=jnp.float32)
                for j in range(first, first + GROUP)
            ]
            for j in range(GROUP):
                target = jobs[batch * BATCH + first + j] & 127
                total[target] += products[j]
        return carry

    lax.fori_loop(0, batches, body, 0)

    def finish(step, carry):
        for j in range(GROUP):
            o = step * GROUP + j
            square = jnp.concatenate([square_a[o], square_b[o]], axis=0)
            out[o] = (3.0 * square - 2.0 * total[o]).T.astype(jnp.bfloat16)
        return carry

    lax.fori_loop(0, out.shape[0] // GROUP, finish, 0)


def cube_part(jobs, count, right_a, right_b, square_a, square_b, pieces_a, pieces_b):
    smem = pl.BlockSpec(memory_space=pltpu.SMEM)
    vmem = pl.BlockSpec(memory_space=pltpu.VMEM)
    anywhere = pl.BlockSpec(memory_space=pl.ANY)
    return pl.pallas_call(
        cube_kernel,
        out_shape=jax.ShapeDtypeStruct((64, 128, 128), jnp.bfloat16),
        in_specs=[smem, smem, anywhere, anywhere, vmem, vmem] + [anywhere] * 20,
        out_specs=vmem,
        scratch_shapes=[
            pltpu.VMEM((2, BATCH, 128, 128), jnp.bfloat16),
            pltpu.VMEM((2, BATCH, 128, 128), jnp.bfloat16),
            pltpu.VMEM((65, 128, 128), jnp.float32),
            pltpu.SemaphoreType.DMA((2,)),
            pltpu.SemaphoreType.DMA((2,)),
        ],
        compiler_params=pltpu.CompilerParams(vmem_limit_bytes=VMEM_LIMIT),
        name="cube_part",
    )(jobs, count, right_a, right_b, square_a, square_b, *pieces_a, *pieces_b)


def packed_jobs(matched, payload):
    total = matched.shape[0]
    ids = jnp.arange(total, dtype=jnp.int32)
    hits = matched.astype(jnp.int32)
    rank = jnp.sum(jnp.where(ids[None, :] < ids[:, None], hits[None, :], 0), axis=1)
    chosen = (rank[None, :] == ids[:, None]) & matched[None, :]
    words = jnp.sum(jnp.where(chosen, payload[None, :], 0), axis=1)
    count = jnp.sum(hits)
    return jnp.where(ids < count, words, 64).astype(jnp.int32), count[None]


def place_of(k):
    group, within = k // 16, k % 16
    y, z_lo, z_hi = group // 8, (group // 4) % 2, group % 4
    return ((y * 4 + z_hi) * 2 + z_lo) * 16 + within


def job_lists(tile_cols, out_cols, layer, group, x, core):
    own_rows = out_cols.shape[0]
    colset = lax.dynamic_index_in_dim(tile_cols, layer, 1, keepdims=False)
    own_cols = lax.dynamic_slice_in_dim(tile_cols, group * own_rows, own_rows, 0)
    wanted = lax.dynamic_index_in_dim(out_cols, layer, 1, keepdims=False)
    through = out_cols.reshape(own_rows, 32)
    every = jnp.arange(tile_cols.shape[0], dtype=jnp.int32)
    rows = jnp.arange(own_rows, dtype=jnp.int32)[:, None]

    def lookup(index):
        return jnp.sum(jnp.where(index[..., None] == every, colset, 0), axis=-1)

    def slots(index):
        same = lookup(index)[:, :, None] == wanted[:, None, :]
        slot = jnp.sum(jnp.where(same, jnp.arange(4, dtype=jnp.int32), 0), axis=-1)
        return jnp.any(same, axis=-1), rows * 4 + slot

    matched, target = slots(own_cols)
    source = rows * 8 + jnp.arange(8, dtype=jnp.int32)[None, :]
    words = (place_of(own_cols) << 14) | (source << 7) | target
    square_jobs = packed_jobs(matched.reshape(-1), words.reshape(-1))

    matched, target = slots(through)
    m = jnp.arange(32, dtype=jnp.int32)[None, :]
    u, t = m // 4, m % 4
    distance = (u // 2 - x) % 4
    half = rows // (own_rows // 2)
    piece = jnp.where(distance == 2, 3 + half, jnp.where(distance == 3, 1, jnp.where(distance == 1, 2, 0)))
    piece = piece + jnp.where(u % 2 == core, 0, 5)
    at = jnp.where(distance == 2, rows % (own_rows // 2), rows) * 4 + t
    words = (place_of(through) << 17) | (piece << 13) | (at << 7) | target
    cube_jobs = packed_jobs(matched.reshape(-1), words.reshape(-1))
    return square_jobs, cube_jobs


def spread(part):
    half = part.shape[0] // 2

    def along_x(block, step):
        return lax.ppermute(block, "x", [(i, (i + step) % 4) for i in range(4)])

    def to_other_core(block):
        return lax.ppermute(block, "core", [(0, 1), (1, 0)])

    below, above = along_x(part, 1), along_x(part, -1)
    far_a, far_b = along_x(below[:half], 1), along_x(above[half:], -1)
    mine = [part, below, above, far_a, far_b]
    return mine + [to_other_core(block) for block in mine]


def on_device(density, tile_cols, out_cols):
    x, core = lax.axis_index("x"), lax.axis_index("core")
    layer = x * 2 + core
    group = lax.axis_index(("y", "z_lo", "z_hi"))
    own_rows = density.shape[0]
    own = jnp.swapaxes(lax.dynamic_index_in_dim(density, layer, 1, keepdims=False), 1, 2)
    own_a, own_b = own[:, :FIRST], own[:, FIRST:]
    right_a = lax.all_gather(own_a, ("y", "z_hi", "z_lo"), axis=0, tiled=True)
    right_b = lax.all_gather(own_b, ("y", "z_hi", "z_lo"), axis=0, tiled=True)
    square_jobs, cube_jobs = job_lists(tile_cols, out_cols, layer, group, x, core)
    left = density.reshape(own_rows * 8, 128, 128)
    square_a, low_a = square_part(*square_jobs, left, right_a)
    pieces_a = spread(low_a)
    square_b, low_b = square_part(*square_jobs, left, right_b)
    pieces_b = spread(low_b)
    purified = cube_part(*cube_jobs, right_a, right_b, square_a, square_b, pieces_a, pieces_b)
    return purified.reshape(own_rows, 1, 4, 128, 128)


def solution(mesh):
    axes = ("y", "z_lo", "z_hi", "x", "core")
    fine = Mesh(mesh.devices.reshape(4, 2, 4, 4, 2), axes)
    rows = ("y", "z_lo", "z_hi")
    return jax.shard_map(
        on_device,
        mesh=fine,
        in_specs=(P(rows, None, None, None), P(), P(rows, None, None)),
        out_specs=P(rows, ("x", "core"), None, None, None),
        check_vma=False,
    )
```

```python
import jax
import jax.numpy as jnp
from jax import lax
from jax.experimental import pallas as pl
from jax.experimental.pallas import tpu as pltpu
from jax.sharding import Mesh
from jax.sharding import PartitionSpec as P

BATCH = 16
PIECES = 14
GROUP = 4
FIRST = 64
VMEM_LIMIT = 60 * 1024 * 1024
TREE = (
    ((-1, 0), (0, 0), (3, 0)),
    ((0, 1), (0, 0), (0, 1)),
    ((1, 0), (0, 0), (1, 0)),
    ((0, -1), (0, 0), (0, 7)),
    ((-1, 0), (0, 7), (3, 7)),
    ((1, 0), (1, 0), (2, 0)),
    ((0, 1), (1, 0), (1, 1)),
    ((0, -1), (0, 7), (0, 6)),
    ((1, 0), (0, 7), (1, 7)),
    ((0, 1), (0, 1), (0, 2)),
    ((0, -1), (0, 6), (0, 5)),
    ((-1, 0), (0, 1), (3, 1)),
    ((1, 0), (1, 1), (2, 1)),
    ((0, 1), (1, 1), (1, 2)),
    ((0, -1), (2, 0), (2, 7)),
    ((-1, 0), (0, 6), (3, 6)),
    ((0, 1), (0, 2), (0, 3)),
    ((0, -1), (1, 7), (1, 6)),
    ((1, 0), (0, 5), (1, 5)),
    ((-1, 0), (0, 2), (3, 2)),
    ((0, 1), (1, 2), (1, 3)),
    ((0, -1), (0, 5), (0, 4)),
    ((-1, 0), (0, 5), (3, 5)),
    ((1, 0), (1, 2), (2, 2)),
    ((1, 0), (1, 5), (2, 5)),
    ((-1, 0), (3, 6), (2, 6)),
    ((0, -1), (1, 5), (1, 4)),
    ((0, 1), (3, 2), (3, 3)),
    ((0, -1), (3, 5), (3, 4)),
    ((0, 1), (2, 2), (2, 3)),
    ((1, 0), (1, 4), (2, 4)),
)
OFFSETS = tuple((dy, dz) for dy in range(4) for dz in range(8))


def run_jobs(jobs, count, left, right, total, left_buf, left_sem, right_buf=None, right_sem=None):
    batches = (count[0] + BATCH - 1) // BATCH
    total[...] = jnp.zeros_like(total)

    def start(batch):
        slot = lax.rem(batch, 2)
        for j in range(BATCH):
            word = jobs[batch * BATCH + j]
            pltpu.make_async_copy(left.at[(word >> 7) & 127], left_buf.at[slot, j], left_sem.at[slot]).start()
            if right_buf is not None:
                pltpu.make_async_copy(right.at[word >> 14], right_buf.at[slot, j], right_sem.at[slot]).start()

    def right_tile(batch, slot, j):
        if right_buf is not None:
            return right_buf[slot, j]
        return right[jobs[batch * BATCH + j] >> 14]

    @pl.when(batches > 0)
    def _():
        start(0)

    def body(batch, carry):
        slot = lax.rem(batch, 2)

        @pl.when(batch + 1 < batches)
        def _():
            start(batch + 1)

        pltpu.make_async_copy(left_buf.at[slot], left_buf.at[slot], left_sem.at[slot]).wait()
        if right_buf is not None:
            pltpu.make_async_copy(right_buf.at[slot], right_buf.at[slot], right_sem.at[slot]).wait()
        for first in range(0, BATCH, GROUP):
            products = [
                lax.dot_general(
                    right_tile(batch, slot, j), left_buf[slot, j], (((1,), (1,)), ((), ())), preferred_element_type=jnp.float32
                )
                for j in range(first, first + GROUP)
            ]
            for j in range(GROUP):
                target = jobs[batch * BATCH + first + j] & 127
                total[target] += products[j]
        return carry

    lax.fori_loop(0, batches, body, 0)


def first_square_kernel(jobs, count, position, left, *refs):
    blocks = refs[: len(OFFSETS)]
    square, square_low, right, held, left_buf, total, left_sem, block_sem, out_sem = refs[len(OFFSETS) :]
    size = blocks[0].shape[0]
    for (dy, dz), block in zip(OFFSETS, blocks, strict=True):
        from_y = (position[0] + (4 - dy)) & 3
        from_z = (position[1] + (8 - dz)) & 7
        pltpu.make_async_copy(block, held.at[pl.ds((from_y * 8 + from_z) * size, size)], block_sem).start()
    pltpu.make_async_copy(held, held, block_sem).wait()
    pltpu.make_async_copy(held, right, out_sem).start()
    run_jobs(jobs, count, left, held, total, left_buf, left_sem)
    square[...] = total[: square.shape[0]]
    square_low[...] = total[: square.shape[0]].astype(jnp.bfloat16)
    pltpu.make_async_copy(held, right, out_sem).wait()


def second_square_kernel(jobs, count, left, right, *refs):
    square, square_low, left_buf, right_buf, total, left_sem, right_sem = refs[-7:]
    run_jobs(jobs, count, left, right, total, left_buf, left_sem, right_buf, right_sem)
    square[...] = total[: square.shape[0]]
    square_low[...] = total[: square.shape[0]].astype(jnp.bfloat16)


def first_square(jobs, count, position, left, blocks):
    size, part = blocks[0].shape[:2]
    smem = pl.BlockSpec(memory_space=pltpu.SMEM)
    vmem = pl.BlockSpec(memory_space=pltpu.VMEM)
    anywhere = pl.BlockSpec(memory_space=pl.ANY)
    return pl.pallas_call(
        first_square_kernel,
        out_shape=(
            jax.ShapeDtypeStruct((64, part, 128), jnp.float32),
            jax.ShapeDtypeStruct((64, part, 128), jnp.bfloat16),
            jax.ShapeDtypeStruct((len(blocks) * size, part, 128), jnp.bfloat16),
        ),
        in_specs=[smem, smem, smem, pl.BlockSpec(memory_space=pltpu.HBM)] + [anywhere] * len(blocks),
        out_specs=(vmem, vmem, pl.BlockSpec(memory_space=pltpu.HBM)),
        scratch_shapes=[
            pltpu.VMEM((len(blocks) * size, part, 128), jnp.bfloat16),
            pltpu.VMEM((2, BATCH, 128, 128), jnp.bfloat16),
            pltpu.VMEM((65, part, 128), jnp.float32),
            pltpu.SemaphoreType.DMA((2,)),
            pltpu.SemaphoreType.DMA,
            pltpu.SemaphoreType.DMA,
        ],
        compiler_params=pltpu.CompilerParams(vmem_limit_bytes=VMEM_LIMIT),
        name="first_square",
    )(jobs, count, position, left, *blocks)


def second_square(jobs, count, left, right, after):
    part = right.shape[1]
    smem = pl.BlockSpec(memory_space=pltpu.SMEM)
    vmem = pl.BlockSpec(memory_space=pltpu.VMEM)
    anywhere = pl.BlockSpec(memory_space=pl.ANY)
    return pl.pallas_call(
        second_square_kernel,
        out_shape=(
            jax.ShapeDtypeStruct((64, part, 128), jnp.float32),
            jax.ShapeDtypeStruct((64, part, 128), jnp.bfloat16),
        ),
        in_specs=[smem, smem] + [pl.BlockSpec(memory_space=pltpu.HBM)] * 2 + [anywhere] * len(after),
        out_specs=(vmem, vmem),
        scratch_shapes=[
            pltpu.VMEM((2, BATCH, 128, 128), jnp.bfloat16),
            pltpu.VMEM((2, BATCH, part, 128), jnp.bfloat16),
            pltpu.VMEM((65, part, 128), jnp.float32),
            pltpu.SemaphoreType.DMA((2,)),
            pltpu.SemaphoreType.DMA((2,)),
        ],
        compiler_params=pltpu.CompilerParams(vmem_limit_bytes=VMEM_LIMIT),
        name="second_square",
    )(jobs, count, left, right, *after)


def cube_kernel(*refs):
    jobs, count, right_a, right_b, square_a, square_b = refs[:6]
    pieces_a, pieces_b = refs[6 : 6 + PIECES], refs[6 + PIECES : 6 + 2 * PIECES]
    out, right_buf, left_buf, total, square, right_sem, left_sem, square_sem = refs[6 + 2 * PIECES :]
    first_part = square_a.shape[1]
    rest = 128 - first_part
    batches = (count[0] + BATCH - 1) // BATCH

    def start(batch):
        slot = lax.rem(batch, 2)
        for j in range(BATCH):
            word = jobs[batch * BATCH + j]
            place = word >> 17
            piece = (word >> 13) & 15
            at = (word >> 7) & 63
            pltpu.make_async_copy(
                right_a.at[place], right_buf.at[slot, j, pl.ds(0, first_part)], right_sem.at[slot]
            ).start()
            pltpu.make_async_copy(
                right_b.at[place], right_buf.at[slot, j, pl.ds(first_part, rest)], right_sem.at[slot]
            ).start()
            for p in range(PIECES):

                @pl.when(piece == p)
                def _(p=p, j=j, at=at):
                    pltpu.make_async_copy(
                        pieces_a[p].at[at], left_buf.at[slot, j, pl.ds(0, first_part)], left_sem.at[slot]
                    ).start()
                    pltpu.make_async_copy(
                        pieces_b[p].at[at], left_buf.at[slot, j, pl.ds(first_part, rest)], left_sem.at[slot]
                    ).start()

    @pl.when(batches > 0)
    def _():
        start(0)

    pltpu.make_async_copy(square_a, square.at[:, pl.ds(0, first_part)], square_sem).start()
    pltpu.make_async_copy(square_b, square.at[:, pl.ds(first_part, rest)], square_sem).start()
    total[...] = jnp.zeros_like(total)

    def body(batch, carry):
        slot = lax.rem(batch, 2)

        @pl.when(batch + 1 < batches)
        def _():
            start(batch + 1)

        pltpu.make_async_copy(right_buf.at[slot], right_buf.at[slot], right_sem.at[slot]).wait()
        pltpu.make_async_copy(left_buf.at[slot], left_buf.at[slot], left_sem.at[slot]).wait()
        for first in range(0, BATCH, GROUP):
            products = [
                jnp.dot(right_buf[slot, j], left_buf[slot, j], preferred_element_type=jnp.float32)
                for j in range(first, first + GROUP)
            ]
            for j in range(GROUP):
                target = jobs[batch * BATCH + first + j] & 127
                total[target] += products[j]
        return carry

    lax.fori_loop(0, batches, body, 0)

    pltpu.make_async_copy(square, square, square_sem).wait()

    def finish(step, carry):
        for j in range(GROUP):
            o = step * GROUP + j
            out[o] = (3.0 * square[o] - 2.0 * total[o]).T.astype(jnp.bfloat16)
        return carry

    lax.fori_loop(0, out.shape[0] // GROUP, finish, 0)


def cube_part(jobs, count, right_a, right_b, square_a, square_b, pieces_a, pieces_b):
    smem = pl.BlockSpec(memory_space=pltpu.SMEM)
    vmem = pl.BlockSpec(memory_space=pltpu.VMEM)
    anywhere = pl.BlockSpec(memory_space=pl.ANY)
    return pl.pallas_call(
        cube_kernel,
        out_shape=jax.ShapeDtypeStruct((64, 128, 128), jnp.bfloat16),
        in_specs=[smem, smem] + [pl.BlockSpec(memory_space=pltpu.HBM)] * 2 + [anywhere] * (2 + 2 * PIECES),
        out_specs=vmem,
        scratch_shapes=[
            pltpu.VMEM((2, BATCH, 128, 128), jnp.bfloat16),
            pltpu.VMEM((2, BATCH, 128, 128), jnp.bfloat16),
            pltpu.VMEM((65, 128, 128), jnp.float32),
            pltpu.VMEM((64, 128, 128), jnp.float32),
            pltpu.SemaphoreType.DMA((2,)),
            pltpu.SemaphoreType.DMA((2,)),
            pltpu.SemaphoreType.DMA,
        ],
        compiler_params=pltpu.CompilerParams(vmem_limit_bytes=VMEM_LIMIT),
        name="cube_part",
    )(jobs, count, right_a, right_b, square_a, square_b, *pieces_a, *pieces_b)


def packed_jobs(matched, payload):
    total = matched.shape[0]
    ids = jnp.arange(total, dtype=jnp.int32)
    hits = matched.astype(jnp.int32)
    rank = jnp.sum(jnp.where(ids[None, :] < ids[:, None], hits[None, :], 0), axis=1)
    chosen = (rank[None, :] == ids[:, None]) & matched[None, :]
    words = jnp.sum(jnp.where(chosen, payload[None, :], 0), axis=1)
    count = jnp.sum(hits)
    return jnp.where(ids < count, words, 64).astype(jnp.int32), count[None]


def place_of(k):
    group, within = k // 16, k % 16
    y, z_lo, z_hi = group // 8, (group // 4) % 2, group % 4
    return ((y * 4 + z_hi) * 2 + z_lo) * 16 + within


def job_lists(tile_cols, out_cols, layer, group, x, core):
    own_rows = out_cols.shape[0]
    colset = lax.dynamic_index_in_dim(tile_cols, layer, 1, keepdims=False)
    own_cols = lax.dynamic_slice_in_dim(tile_cols, group * own_rows, own_rows, 0)
    wanted = lax.dynamic_index_in_dim(out_cols, layer, 1, keepdims=False)
    through = out_cols.reshape(own_rows, 32)
    every = jnp.arange(tile_cols.shape[0], dtype=jnp.int32)
    rows = jnp.arange(own_rows, dtype=jnp.int32)[:, None]

    def lookup(index):
        return jnp.sum(jnp.where(index[..., None] == every, colset, 0), axis=-1)

    def slots(index):
        same = lookup(index)[:, :, None] == wanted[:, None, :]
        slot = jnp.sum(jnp.where(same, jnp.arange(4, dtype=jnp.int32), 0), axis=-1)
        return jnp.any(same, axis=-1), rows * 4 + slot

    matched, target = slots(own_cols)
    source = rows * 8 + jnp.arange(8, dtype=jnp.int32)[None, :]
    words = (place_of(own_cols) << 14) | (source << 7) | target
    square_jobs = packed_jobs(matched.reshape(-1), words.reshape(-1))

    matched, target = slots(through)
    m = jnp.arange(32, dtype=jnp.int32)[None, :]
    u, t = m // 4, m % 4
    distance = (u // 2 - x) % 4
    half = rows // (own_rows // 2)
    piece = jnp.where(distance == 0, 0, jnp.where(distance == 3, 1, jnp.where(distance == 1, 3, 5)) + half)
    piece = piece + jnp.where(u % 2 == core, 0, PIECES // 2)
    at = jnp.where(distance == 0, rows, rows % (own_rows // 2)) * 4 + t
    words = (place_of(through) << 17) | (piece << 13) | (at << 7) | target
    cube_jobs = packed_jobs(matched.reshape(-1), words.reshape(-1))
    return square_jobs, cube_jobs


def tree_gather(own):
    ring = [(z % 2) * 4 + z // 2 for z in range(8)]
    held = {(0, 0): own}
    for (dy, dz), source, target in TREE:
        if dy:
            held[target] = lax.ppermute(held[source], "y", [(i, (i + dy) % 4) for i in range(4)])
        else:
            steps = [(ring[z], ring[(z + dz) % 8]) for z in range(8)]
            held[target] = lax.ppermute(held[source], ("z_lo", "z_hi"), steps)
    return [held[offset] for offset in OFFSETS]


def spread(part):
    half = part.shape[0] // 2

    def along_x(block, step):
        return lax.ppermute(block, "x", [(i, (i + step) % 4) for i in range(4)])

    def to_other_core(block):
        return lax.ppermute(block, "core", [(0, 1), (1, 0)])

    low, high = part[:half], part[half:]
    below_low, above_high = along_x(low, 1), along_x(high, -1)
    below_high, above_low = along_x(high, 1), along_x(low, -1)
    far_low, far_high = along_x(below_low, 1), along_x(above_high, -1)
    mine = [part, below_low, below_high, above_low, above_high, far_low, far_high]
    return mine + [to_other_core(block) for block in mine]


def on_device(density, tile_cols, out_cols):
    x, core = lax.axis_index("x"), lax.axis_index("core")
    layer = x * 2 + core
    group = lax.axis_index(("y", "z_lo", "z_hi"))
    own_rows = density.shape[0]
    own = jnp.swapaxes(lax.dynamic_index_in_dim(density, layer, 1, keepdims=False), 1, 2)
    own_a, own_b = own[:, :FIRST], own[:, FIRST:]
    right_b = lax.all_gather(own_b, ("y", "z_hi", "z_lo"), axis=0, tiled=True)
    blocks = tree_gather(own_a)
    square_jobs, cube_jobs = job_lists(tile_cols, out_cols, layer, group, x, core)
    position = jnp.stack([lax.axis_index("y"), lax.axis_index("z_hi") * 2 + lax.axis_index("z_lo")]).astype(jnp.int32)
    left = density.reshape(own_rows * 8, 128, 128)
    square_a, low_a, right_a = first_square(*square_jobs, position, left, blocks)
    pieces_a = spread(low_a)
    square_b, low_b = second_square(*square_jobs, left, right_b, pieces_a[1:5])
    pieces_b = spread(low_b)
    purified = cube_part(*cube_jobs, right_a, right_b, square_a, square_b, pieces_a, pieces_b)
    return purified.reshape(own_rows, 1, 4, 128, 128)


def solution(mesh):
    axes = ("y", "z_lo", "z_hi", "x", "core")
    fine = Mesh(mesh.devices.reshape(4, 2, 4, 4, 2), axes)
    rows = ("y", "z_lo", "z_hi")
    return jax.shard_map(
        on_device,
        mesh=fine,
        in_specs=(P(rows, None, None, None), P(), P(rows, None, None)),
        out_specs=P(rows, ("x", "core"), None, None, None),
        check_vma=False,
    )
```

```python
import jax
import jax.numpy as jnp
from jax import lax
from jax.experimental import pallas as pl
from jax.experimental.pallas import tpu as pltpu
from jax.sharding import Mesh
from jax.sharding import PartitionSpec as P

PIECES = 16
GROUP = 4
FIRST = 48
VMEM_LIMIT = 60 * 1024 * 1024
TREE = (
    ((-1, 0), (0, 0), (3, 0)),
    ((0, 1), (0, 0), (0, 1)),
    ((1, 0), (0, 0), (1, 0)),
    ((0, -1), (0, 0), (0, 7)),
    ((-1, 0), (0, 7), (3, 7)),
    ((1, 0), (1, 0), (2, 0)),
    ((0, 1), (1, 0), (1, 1)),
    ((0, -1), (0, 7), (0, 6)),
    ((1, 0), (0, 7), (1, 7)),
    ((0, 1), (0, 1), (0, 2)),
    ((0, -1), (0, 6), (0, 5)),
    ((-1, 0), (0, 1), (3, 1)),
    ((1, 0), (1, 1), (2, 1)),
    ((0, 1), (1, 1), (1, 2)),
    ((0, -1), (2, 0), (2, 7)),
    ((-1, 0), (0, 6), (3, 6)),
    ((0, 1), (0, 2), (0, 3)),
    ((0, -1), (1, 7), (1, 6)),
    ((1, 0), (0, 5), (1, 5)),
    ((-1, 0), (0, 2), (3, 2)),
    ((0, 1), (1, 2), (1, 3)),
    ((0, -1), (0, 5), (0, 4)),
    ((-1, 0), (0, 5), (3, 5)),
    ((1, 0), (1, 2), (2, 2)),
    ((1, 0), (1, 5), (2, 5)),
    ((-1, 0), (3, 6), (2, 6)),
    ((0, -1), (1, 5), (1, 4)),
    ((0, 1), (3, 2), (3, 3)),
    ((0, -1), (3, 5), (3, 4)),
    ((0, 1), (2, 2), (2, 3)),
    ((1, 0), (1, 4), (2, 4)),
)
OFFSETS = tuple((dy, dz) for dy in range(4) for dz in range(8))


def add_products(jobs, count, total, product):
    def body(step, carry):
        first = step * GROUP
        products = [product(first + j) for j in range(GROUP)]
        for j in range(GROUP):
            total[jobs[first + j] & 127] += products[j]
        return carry

    lax.fori_loop(0, (count + GROUP - 1) // GROUP, body, 0)


def square_jobs_run(jobs, count, left, right, total, left_buf, left_sem, right_buf=None, right_sem=None):
    def start(j, carry):
        word = jobs[j]
        pltpu.make_async_copy(left.at[(word >> 7) & 127], left_buf.at[j], left_sem).start()
        if right_buf is not None:
            pltpu.make_async_copy(right.at[word >> 14], right_buf.at[j], right_sem).start()
        return carry

    def wait(j, carry):
        pltpu.make_async_copy(left.at[0], left_buf.at[j], left_sem).wait()
        if right_buf is not None:
            pltpu.make_async_copy(right.at[0], right_buf.at[j], right_sem).wait()
        return carry

    def product(j):
        right_tile = right[jobs[j] >> 14] if right_buf is None else right_buf[j]
        return lax.dot_general(right_tile, left_buf[j], (((1,), (1,)), ((), ())), preferred_element_type=jnp.float32)

    lax.fori_loop(0, count, start, 0)
    total[...] = jnp.zeros_like(total)
    lax.fori_loop(0, count, wait, 0)
    add_products(jobs, count, total, product)


def write_square(total, square, parts, out_sem):
    copy = pltpu.make_async_copy(total.at[pl.ds(0, square.shape[0])], square, out_sem)
    copy.start()
    first = 0
    for part in parts:
        part[...] = total[first : first + part.shape[0]].astype(jnp.bfloat16)
        first += part.shape[0]
    copy.wait()


def first_square_kernel(jobs, count, position, left, *refs):
    blocks = refs[: len(OFFSETS)]
    square, whole, right, held, left_buf, total, left_sem, block_sem, right_sem, out_sem = refs[-10:]
    size = blocks[0].shape[0]
    for (dy, dz), block in zip(OFFSETS, blocks, strict=True):
        from_y = (position[0] + (4 - dy)) & 3
        from_z = (position[1] + (8 - dz)) & 7
        pltpu.make_async_copy(block, held.at[pl.ds((from_y * 8 + from_z) * size, size)], block_sem).start()
    pltpu.make_async_copy(held, held, block_sem).wait()
    pltpu.make_async_copy(held, right, right_sem).start()
    square_jobs_run(jobs, count[0], left, held, total, left_buf, left_sem)
    write_square(total, square, [whole], out_sem)
    pltpu.make_async_copy(held, right, right_sem).wait()


def second_square_kernel(jobs, count, left, right, *refs):
    square, low, high, left_buf, right_buf, total, left_sem, right_sem, out_sem = refs[-9:]
    square_jobs_run(jobs, count[0], left, right, total, left_buf, left_sem, right_buf, right_sem)
    write_square(total, square, [low, high], out_sem)


SMEM = pl.BlockSpec(memory_space=pltpu.SMEM)
VMEM = pl.BlockSpec(memory_space=pltpu.VMEM)
HBM = pl.BlockSpec(memory_space=pltpu.HBM)


def square_outs(part, cuts):
    low = jax.ShapeDtypeStruct((64 // cuts, part, 128), jnp.bfloat16)
    return (jax.ShapeDtypeStruct((64, part, 128), jnp.float32),) + (low,) * cuts


def first_square(jobs, count, position, left, blocks, after):
    size, part = blocks[0].shape[:2]
    return pl.pallas_call(
        first_square_kernel,
        out_shape=square_outs(part, 1) + (jax.ShapeDtypeStruct((len(blocks) * size, part, 128), jnp.bfloat16),),
        in_specs=[SMEM, SMEM, SMEM] + [HBM] * (1 + len(blocks) + len(after)),
        out_specs=(HBM, VMEM, HBM),
        scratch_shapes=[
            pltpu.VMEM((len(blocks) * size, part, 128), jnp.bfloat16),
            pltpu.VMEM((jobs.shape[0], 128, 128), jnp.bfloat16),
            pltpu.VMEM((65, part, 128), jnp.float32),
            pltpu.SemaphoreType.DMA,
            pltpu.SemaphoreType.DMA,
            pltpu.SemaphoreType.DMA,
            pltpu.SemaphoreType.DMA,
        ],
        compiler_params=pltpu.CompilerParams(vmem_limit_bytes=VMEM_LIMIT),
        name="first_square",
    )(jobs, count, position, left, *blocks, *after)


def second_square(jobs, count, left, right):
    part = right.shape[1]
    return pl.pallas_call(
        second_square_kernel,
        out_shape=square_outs(part, 2),
        in_specs=[SMEM, SMEM, HBM, HBM],
        out_specs=(HBM, VMEM, VMEM),
        scratch_shapes=[
            pltpu.VMEM((jobs.shape[0], 128, 128), jnp.bfloat16),
            pltpu.VMEM((jobs.shape[0], part, 128), jnp.bfloat16),
            pltpu.VMEM((65, part, 128), jnp.float32),
            pltpu.SemaphoreType.DMA,
            pltpu.SemaphoreType.DMA,
            pltpu.SemaphoreType.DMA,
        ],
        compiler_params=pltpu.CompilerParams(vmem_limit_bytes=VMEM_LIMIT),
        name="second_square",
    )(jobs, count, left, right)


def cube_kernel(*refs):
    jobs, bounds, right_a, right_b, square_a, square_b = refs[:6]
    pieces_a, pieces_b = refs[6:16], refs[16 : 16 + PIECES]
    out, right_buf, left_buf, total, square, right_sem, left_sem, square_sem = refs[16 + PIECES :]
    first_part = square_a.shape[1]
    rest = 128 - first_part
    count = bounds[PIECES]
    for p in range(PIECES):
        kind, half = p % 8 // 2, p % 2
        whole = kind < 3
        piece_a = pieces_a[p // 8 * 5 + (kind if whole else 3 + half)]
        shift = 32 * half if whole else 0

        def start(j, carry, p=p, piece_a=piece_a, shift=shift):
            word = jobs[j]
            place = word >> 17
            at = (word >> 7) & 63
            top, bottom = pl.ds(0, first_part), pl.ds(first_part, rest)
            pltpu.make_async_copy(piece_a.at[at + shift], left_buf.at[j, top], left_sem).start()
            pltpu.make_async_copy(pieces_b[p].at[at], left_buf.at[j, bottom], left_sem).start()
            pltpu.make_async_copy(right_a.at[place], right_buf.at[j, top], right_sem).start()
            pltpu.make_async_copy(right_b.at[place], right_buf.at[j, bottom], right_sem).start()
            return carry

        lax.fori_loop(bounds[p], bounds[p + 1], start, 0)
    pltpu.make_async_copy(square_a, square.at[:, pl.ds(0, first_part)], square_sem).start()
    pltpu.make_async_copy(square_b, square.at[:, pl.ds(first_part, rest)], square_sem).start()
    total[...] = jnp.zeros_like(total)

    def wait(j, carry):
        pltpu.make_async_copy(left_buf.at[j], left_buf.at[j], left_sem).wait()
        pltpu.make_async_copy(right_buf.at[j], right_buf.at[j], right_sem).wait()
        return carry

    def product(j):
        return jnp.dot(right_buf[j], left_buf[j], preferred_element_type=jnp.float32)

    lax.fori_loop(0, count, wait, 0)
    add_products(jobs, count, total, product)
    pltpu.make_async_copy(square, square, square_sem).wait()

    def finish(step, carry):
        for j in range(GROUP):
            o = step * GROUP + j
            out[o] = (3.0 * square[o] - 2.0 * total[o]).T.astype(jnp.bfloat16)
        return carry

    lax.fori_loop(0, out.shape[0] // GROUP, finish, 0)


def cube_part(jobs, bounds, right_a, right_b, square_a, square_b, pieces_a, pieces_b):
    return pl.pallas_call(
        cube_kernel,
        out_shape=jax.ShapeDtypeStruct((64, 128, 128), jnp.bfloat16),
        in_specs=[SMEM, SMEM] + [HBM] * (14 + PIECES),
        out_specs=VMEM,
        scratch_shapes=[
            pltpu.VMEM((jobs.shape[0], 128, 128), jnp.bfloat16),
            pltpu.VMEM((jobs.shape[0], 128, 128), jnp.bfloat16),
            pltpu.VMEM((65, 128, 128), jnp.float32),
            pltpu.VMEM((64, 128, 128), jnp.float32),
            pltpu.SemaphoreType.DMA,
            pltpu.SemaphoreType.DMA,
            pltpu.SemaphoreType.DMA,
        ],
        compiler_params=pltpu.CompilerParams(vmem_limit_bytes=VMEM_LIMIT),
        name="cube_part",
    )(jobs, bounds, right_a, right_b, square_a, square_b, *pieces_a, *pieces_b)


def packed_jobs(matched, payload, kind):
    total = matched.shape[0]
    ids = jnp.arange(total, dtype=jnp.int32)
    order = kind * total + ids
    hits = matched.astype(jnp.int32)
    rank = jnp.sum(jnp.where(order[None, :] < order[:, None], hits[None, :], 0), axis=1)
    chosen = (rank[None, :] == ids[:, None]) & matched[None, :]
    words = jnp.sum(jnp.where(chosen, payload[None, :], 0), axis=1)
    count = jnp.sum(hits)
    return jnp.where(ids < count, words, 64).astype(jnp.int32), count[None]


def place_of(k):
    group, within = k // 16, k % 16
    y, z_lo, z_hi = group // 8, (group // 4) % 2, group % 4
    return ((y * 4 + z_hi) * 2 + z_lo) * 16 + within


def job_lists(tile_cols, out_cols, layer, group, x, core):
    own_rows = out_cols.shape[0]
    colset = lax.dynamic_index_in_dim(tile_cols, layer, 1, keepdims=False)
    own_cols = lax.dynamic_slice_in_dim(tile_cols, group * own_rows, own_rows, 0)
    wanted = lax.dynamic_index_in_dim(out_cols, layer, 1, keepdims=False)
    through = out_cols.reshape(own_rows, 32)
    every = jnp.arange(tile_cols.shape[0], dtype=jnp.int32)
    rows = jnp.arange(own_rows, dtype=jnp.int32)[:, None]

    def lookup(index):
        return jnp.sum(jnp.where(index[..., None] == every, colset, 0), axis=-1)

    def slots(index):
        same = lookup(index)[:, :, None] == wanted[:, None, :]
        slot = jnp.sum(jnp.where(same, jnp.arange(4, dtype=jnp.int32), 0), axis=-1)
        return jnp.any(same, axis=-1), rows * 4 + slot

    matched, target = slots(own_cols)
    source = rows * 8 + jnp.arange(8, dtype=jnp.int32)[None, :]
    words = (place_of(own_cols) << 14) | (source << 7) | target
    square_jobs = packed_jobs(matched.reshape(-1), words.reshape(-1), 0)

    matched, target = slots(through)
    m = jnp.arange(32, dtype=jnp.int32)[None, :]
    u, t = m // 4, m % 4
    distance = (u // 2 - x) % 4
    half = rows // (own_rows // 2)
    piece = jnp.where(distance == 3, 2, jnp.where(distance == 1, 4, jnp.where(distance == 2, 6, 0))) + half
    piece = piece + jnp.where(u % 2 == core, 0, PIECES // 2)
    at = rows % (own_rows // 2) * 4 + t
    words = (place_of(through) << 17) | (piece << 13) | (at << 7) | target
    matched, piece = matched.reshape(-1), piece.reshape(-1)
    jobs, _ = packed_jobs(matched, words.reshape(-1), piece)
    below = piece[None, :] < jnp.arange(PIECES + 1, dtype=jnp.int32)[:, None]
    bounds = jnp.sum((below & matched[None, :]).astype(jnp.int32), axis=1)
    cube_jobs = (jobs, bounds)
    return square_jobs, cube_jobs


def tree_gather(own):
    ring = [(z % 2) * 4 + z // 2 for z in range(8)]
    held = {(0, 0): own}
    for (dy, dz), source, target in TREE:
        if dy:
            held[target] = lax.ppermute(held[source], "y", [(i, (i + dy) % 4) for i in range(4)])
        else:
            steps = [(ring[z], ring[(z + dz) % 8]) for z in range(8)]
            held[target] = lax.ppermute(held[source], ("z_lo", "z_hi"), steps)
    return [held[offset] for offset in OFFSETS]


def along_x(block, step):
    return lax.ppermute(block, "x", [(i, (i + step) % 4) for i in range(4)])


def to_other_core(block):
    return lax.ppermute(block, "core", [(0, 1), (1, 0)])


def spread_first(whole):
    half = whole.shape[0] // 2
    below, above = along_x(whole, 1), along_x(whole, -1)
    return [whole, below, above, along_x(below[:half], 1), along_x(above[half:], -1)]


def spread_second(low, high):
    below_low, above_high = along_x(low, 1), along_x(high, -1)
    below_high, above_low = along_x(high, 1), along_x(low, -1)
    far_low, far_high = along_x(below_low, 1), along_x(above_high, -1)
    mine = [low, high, below_low, below_high, above_low, above_high, far_low, far_high]
    late_low, _ = lax.optimization_barrier((low, below_low))
    late_high, _ = lax.optimization_barrier((high, above_high))
    return mine + [to_other_core(block) for block in [late_low, late_high] + mine[2:]]


def on_device(density, tile_cols, out_cols):
    x, core = lax.axis_index("x"), lax.axis_index("core")
    layer = x * 2 + core
    group = lax.axis_index(("y", "z_lo", "z_hi"))
    own_rows = density.shape[0]
    own = jnp.swapaxes(lax.dynamic_index_in_dim(density, layer, 1, keepdims=False), 1, 2)
    own_a, own_b = own[:, :FIRST], own[:, FIRST:]
    right_b = lax.all_gather(own_b, ("y", "z_hi", "z_lo"), axis=0, tiled=True)
    blocks = tree_gather(own_a)
    square_jobs, cube_jobs = job_lists(tile_cols, out_cols, layer, group, x, core)
    position = jnp.stack([lax.axis_index("y"), lax.axis_index("z_hi") * 2 + lax.axis_index("z_lo")]).astype(jnp.int32)
    left = density.reshape(own_rows * 8, 128, 128)
    square_a, whole_a, right_a = first_square(*square_jobs, position, left, blocks, cube_jobs)
    mine_a = spread_first(whole_a)
    square_b, low_b, high_b = second_square(*square_jobs, left, right_b)
    pieces_a = mine_a + [to_other_core(lax.optimization_barrier((block, low_b))[0]) for block in mine_a]
    pieces_b = spread_second(low_b, high_b)
    purified = cube_part(*cube_jobs, right_a, right_b, square_a, square_b, pieces_a, pieces_b)
    return purified.reshape(own_rows, 1, 4, 128, 128)


def solution(mesh):
    axes = ("y", "z_lo", "z_hi", "x", "core")
    fine = Mesh(mesh.devices.reshape(4, 2, 4, 4, 2), axes)
    rows = ("y", "z_lo", "z_hi")
    return jax.shard_map(
        on_device,
        mesh=fine,
        in_specs=(P(rows, None, None, None), P(), P(rows, None, None)),
        out_specs=P(rows, ("x", "core"), None, None, None),
        check_vma=False,
    )
```

```python
import jax
import jax.numpy as jnp
from jax import lax
from jax.experimental import pallas as pl
from jax.experimental.pallas import tpu as pltpu
from jax.sharding import Mesh
from jax.sharding import PartitionSpec as P

PIECES = 16
GROUP = 4
FIRST = 48
VMEM_LIMIT = 60 * 1024 * 1024
TREE = (
    ((-1, 0), (0, 0), (3, 0)),
    ((0, 1), (0, 0), (0, 1)),
    ((1, 0), (0, 0), (1, 0)),
    ((0, -1), (0, 0), (0, 7)),
    ((-1, 0), (0, 7), (3, 7)),
    ((1, 0), (1, 0), (2, 0)),
    ((0, 1), (1, 0), (1, 1)),
    ((0, -1), (0, 7), (0, 6)),
    ((1, 0), (0, 7), (1, 7)),
    ((0, 1), (0, 1), (0, 2)),
    ((0, -1), (0, 6), (0, 5)),
    ((-1, 0), (0, 1), (3, 1)),
    ((1, 0), (1, 1), (2, 1)),
    ((0, 1), (1, 1), (1, 2)),
    ((0, -1), (2, 0), (2, 7)),
    ((-1, 0), (0, 6), (3, 6)),
    ((0, 1), (0, 2), (0, 3)),
    ((0, -1), (1, 7), (1, 6)),
    ((1, 0), (0, 5), (1, 5)),
    ((-1, 0), (0, 2), (3, 2)),
    ((0, 1), (1, 2), (1, 3)),
    ((0, -1), (0, 5), (0, 4)),
    ((-1, 0), (0, 5), (3, 5)),
    ((1, 0), (1, 2), (2, 2)),
    ((1, 0), (1, 5), (2, 5)),
    ((-1, 0), (3, 6), (2, 6)),
    ((0, -1), (1, 5), (1, 4)),
    ((0, 1), (3, 2), (3, 3)),
    ((0, -1), (3, 5), (3, 4)),
    ((0, 1), (2, 2), (2, 3)),
    ((1, 0), (1, 4), (2, 4)),
)
OFFSETS = tuple((dy, dz) for dy in range(4) for dz in range(8))


def add_products(jobs, count, total, product):
    def body(step, carry):
        first = step * GROUP
        products = [product(first + j) for j in range(GROUP)]
        for j in range(GROUP):
            total[jobs[first + j] & 127] += products[j]
        return carry

    lax.fori_loop(0, (count + GROUP - 1) // GROUP, body, 0)


def square_jobs_run(jobs, count, left, right, total, left_buf, left_sem, right_buf=None, right_sem=None):
    def start(j, carry):
        word = jobs[j]
        pltpu.make_async_copy(left.at[(word >> 7) & 127], left_buf.at[j], left_sem).start()
        if right_buf is not None:
            pltpu.make_async_copy(right.at[word >> 14], right_buf.at[j], right_sem).start()
        return carry

    def wait(j, carry):
        pltpu.make_async_copy(left.at[0], left_buf.at[j], left_sem).wait()
        if right_buf is not None:
            pltpu.make_async_copy(right.at[0], right_buf.at[j], right_sem).wait()
        return carry

    def product(j):
        right_tile = right[jobs[j] >> 14] if right_buf is None else right_buf[j]
        return lax.dot_general(right_tile, left_buf[j], (((1,), (1,)), ((), ())), preferred_element_type=jnp.float32)

    lax.fori_loop(0, count, start, 0)
    total[...] = jnp.zeros_like(total)
    lax.fori_loop(0, count, wait, 0)
    add_products(jobs, count, total, product)


def write_square(total, square, parts, out_sem):
    copy = pltpu.make_async_copy(total.at[pl.ds(0, square.shape[0])], square, out_sem)
    copy.start()
    first = 0
    for part in parts:
        part[...] = total[first : first + part.shape[0]].astype(jnp.bfloat16)
        first += part.shape[0]
    copy.wait()


def first_square_kernel(jobs, count, position, left, *refs):
    blocks = refs[: len(OFFSETS)]
    square, whole, right, held, left_buf, total, left_sem, block_sem, right_sem, out_sem = refs[-10:]
    size = blocks[0].shape[0]
    for (dy, dz), block in zip(OFFSETS, blocks, strict=True):
        from_y = (position[0] + (4 - dy)) & 3
        from_z = (position[1] + (8 - dz)) & 7
        pltpu.make_async_copy(block, held.at[pl.ds((from_y * 8 + from_z) * size, size)], block_sem).start()
    pltpu.make_async_copy(held, held, block_sem).wait()
    pltpu.make_async_copy(held, right, right_sem).start()
    square_jobs_run(jobs, count[0], left, held, total, left_buf, left_sem)
    write_square(total, square, [whole], out_sem)
    pltpu.make_async_copy(held, right, right_sem).wait()


def second_square_kernel(jobs, count, left, right, *refs):
    square, low, high, left_buf, right_buf, total, left_sem, right_sem, out_sem = refs[-9:]
    square_jobs_run(jobs, count[0], left, right, total, left_buf, left_sem, right_buf, right_sem)
    write_square(total, square, [low, high], out_sem)


SMEM = pl.BlockSpec(memory_space=pltpu.SMEM)
VMEM = pl.BlockSpec(memory_space=pltpu.VMEM)
HBM = pl.BlockSpec(memory_space=pltpu.HBM)


def square_outs(part, cuts):
    low = jax.ShapeDtypeStruct((64 // cuts, part, 128), jnp.bfloat16)
    return (jax.ShapeDtypeStruct((64, part, 128), jnp.float32),) + (low,) * cuts


def first_square(jobs, count, position, left, blocks, after):
    size, part = blocks[0].shape[:2]
    return pl.pallas_call(
        first_square_kernel,
        out_shape=square_outs(part, 1) + (jax.ShapeDtypeStruct((len(blocks) * size, part, 128), jnp.bfloat16),),
        in_specs=[SMEM, SMEM, SMEM] + [HBM] * (1 + len(blocks) + len(after)),
        out_specs=(HBM, VMEM, HBM),
        scratch_shapes=[
            pltpu.VMEM((len(blocks) * size, part, 128), jnp.bfloat16),
            pltpu.VMEM((jobs.shape[0], 128, 128), jnp.bfloat16),
            pltpu.VMEM((65, part, 128), jnp.float32),
            pltpu.SemaphoreType.DMA,
            pltpu.SemaphoreType.DMA,
            pltpu.SemaphoreType.DMA,
            pltpu.SemaphoreType.DMA,
        ],
        compiler_params=pltpu.CompilerParams(vmem_limit_bytes=VMEM_LIMIT),
        name="first_square",
    )(jobs, count, position, left, *blocks, *after)


def second_square(jobs, count, left, right, after):
    part = right.shape[1]
    return pl.pallas_call(
        second_square_kernel,
        out_shape=square_outs(part, 2),
        in_specs=[SMEM, SMEM, HBM, HBM] + [HBM] * len(after),
        out_specs=(HBM, VMEM, VMEM),
        scratch_shapes=[
            pltpu.VMEM((jobs.shape[0], 128, 128), jnp.bfloat16),
            pltpu.VMEM((jobs.shape[0], part, 128), jnp.bfloat16),
            pltpu.VMEM((65, part, 128), jnp.float32),
            pltpu.SemaphoreType.DMA,
            pltpu.SemaphoreType.DMA,
            pltpu.SemaphoreType.DMA,
        ],
        compiler_params=pltpu.CompilerParams(vmem_limit_bytes=VMEM_LIMIT),
        name="second_square",
    )(jobs, count, left, right, *after)


def cube_kernel(*refs):
    jobs, bounds, right_a, right_b, square_a, square_b = refs[:6]
    pieces_a, pieces_b = refs[6:16], refs[16 : 16 + PIECES]
    out, right_buf, left_buf, total, square, right_sem, left_sem, square_sem = refs[16 + PIECES :]
    first_part = square_a.shape[1]
    rest = 128 - first_part
    count = bounds[PIECES]
    for p in range(PIECES):
        kind, half = p % 8 // 2, p % 2
        whole = kind < 3
        piece_a = pieces_a[p // 8 * 5 + (kind if whole else 3 + half)]
        shift = 32 * half if whole else 0

        def start(j, carry, p=p, piece_a=piece_a, shift=shift):
            word = jobs[j]
            place = word >> 17
            at = (word >> 7) & 63
            top, bottom = pl.ds(0, first_part), pl.ds(first_part, rest)
            pltpu.make_async_copy(piece_a.at[at + shift], left_buf.at[j, top], left_sem).start()
            pltpu.make_async_copy(pieces_b[p].at[at], left_buf.at[j, bottom], left_sem).start()
            pltpu.make_async_copy(right_a.at[place], right_buf.at[j, top], right_sem).start()
            pltpu.make_async_copy(right_b.at[place], right_buf.at[j, bottom], right_sem).start()
            return carry

        lax.fori_loop(bounds[p], bounds[p + 1], start, 0)
    pltpu.make_async_copy(square_a, square.at[:, pl.ds(0, first_part)], square_sem).start()
    pltpu.make_async_copy(square_b, square.at[:, pl.ds(first_part, rest)], square_sem).start()
    total[...] = jnp.zeros_like(total)

    def wait(j, carry):
        pltpu.make_async_copy(left_buf.at[j], left_buf.at[j], left_sem).wait()
        pltpu.make_async_copy(right_buf.at[j], right_buf.at[j], right_sem).wait()
        return carry

    def product(j):
        return jnp.dot(right_buf[j], left_buf[j], preferred_element_type=jnp.float32)

    lax.fori_loop(0, count, wait, 0)
    add_products(jobs, count, total, product)
    pltpu.make_async_copy(square, square, square_sem).wait()

    def finish(step, carry):
        for j in range(GROUP):
            o = step * GROUP + j
            out[o] = (3.0 * square[o] - 2.0 * total[o]).T.astype(jnp.bfloat16)
        return carry

    lax.fori_loop(0, out.shape[0] // GROUP, finish, 0)


def cube_part(jobs, bounds, right_a, right_b, square_a, square_b, pieces_a, pieces_b):
    return pl.pallas_call(
        cube_kernel,
        out_shape=jax.ShapeDtypeStruct((64, 128, 128), jnp.bfloat16),
        in_specs=[SMEM, SMEM] + [HBM] * (14 + PIECES),
        out_specs=VMEM,
        scratch_shapes=[
            pltpu.VMEM((jobs.shape[0], 128, 128), jnp.bfloat16),
            pltpu.VMEM((jobs.shape[0], 128, 128), jnp.bfloat16),
            pltpu.VMEM((65, 128, 128), jnp.float32),
            pltpu.VMEM((64, 128, 128), jnp.float32),
            pltpu.SemaphoreType.DMA,
            pltpu.SemaphoreType.DMA,
            pltpu.SemaphoreType.DMA,
        ],
        compiler_params=pltpu.CompilerParams(vmem_limit_bytes=VMEM_LIMIT),
        name="cube_part",
    )(jobs, bounds, right_a, right_b, square_a, square_b, *pieces_a, *pieces_b)


def packed_jobs(matched, payload, kind):
    total = matched.shape[0]
    ids = jnp.arange(total, dtype=jnp.int32)
    order = kind * total + ids
    hits = matched.astype(jnp.int32)
    rank = jnp.sum(jnp.where(order[None, :] < order[:, None], hits[None, :], 0), axis=1)
    chosen = (rank[None, :] == ids[:, None]) & matched[None, :]
    words = jnp.sum(jnp.where(chosen, payload[None, :], 0), axis=1)
    count = jnp.sum(hits)
    return jnp.where(ids < count, words, 64).astype(jnp.int32), count[None]


def place_of(k):
    group, within = k // 16, k % 16
    y, z_lo, z_hi = group // 8, (group // 4) % 2, group % 4
    return ((y * 4 + z_hi) * 2 + z_lo) * 16 + within


def job_lists(tile_cols, out_cols, layer, group, x, core):
    own_rows = out_cols.shape[0]
    colset = lax.dynamic_index_in_dim(tile_cols, layer, 1, keepdims=False)
    own_cols = lax.dynamic_slice_in_dim(tile_cols, group * own_rows, own_rows, 0)
    wanted = lax.dynamic_index_in_dim(out_cols, layer, 1, keepdims=False)
    through = out_cols.reshape(own_rows, 32)
    every = jnp.arange(tile_cols.shape[0], dtype=jnp.int32)
    rows = jnp.arange(own_rows, dtype=jnp.int32)[:, None]

    def lookup(index):
        return jnp.sum(jnp.where(index[..., None] == every, colset, 0), axis=-1)

    def slots(index):
        same = lookup(index)[:, :, None] == wanted[:, None, :]
        slot = jnp.sum(jnp.where(same, jnp.arange(4, dtype=jnp.int32), 0), axis=-1)
        return jnp.any(same, axis=-1), rows * 4 + slot

    matched, target = slots(own_cols)
    source = rows * 8 + jnp.arange(8, dtype=jnp.int32)[None, :]
    words = (place_of(own_cols) << 14) | (source << 7) | target
    square_jobs = packed_jobs(matched.reshape(-1), words.reshape(-1), 0)

    matched, target = slots(through)
    m = jnp.arange(32, dtype=jnp.int32)[None, :]
    u, t = m // 4, m % 4
    distance = (u // 2 - x) % 4
    half = rows // (own_rows // 2)
    piece = jnp.where(distance == 3, 2, jnp.where(distance == 1, 4, jnp.where(distance == 2, 6, 0))) + half
    piece = piece + jnp.where(u % 2 == core, 0, PIECES // 2)
    at = rows % (own_rows // 2) * 4 + t
    words = (place_of(through) << 17) | (piece << 13) | (at << 7) | target
    matched, piece = matched.reshape(-1), piece.reshape(-1)
    jobs, _ = packed_jobs(matched, words.reshape(-1), piece)
    below = piece[None, :] < jnp.arange(PIECES + 1, dtype=jnp.int32)[:, None]
    bounds = jnp.sum((below & matched[None, :]).astype(jnp.int32), axis=1)
    cube_jobs = (jobs, bounds)
    return square_jobs, cube_jobs


def tree_gather(own):
    ring = [(z % 2) * 4 + z // 2 for z in range(8)]
    held = {(0, 0): own}
    for (dy, dz), source, target in TREE:
        if dy:
            held[target] = lax.ppermute(held[source], "y", [(i, (i + dy) % 4) for i in range(4)])
        else:
            steps = [(ring[z], ring[(z + dz) % 8]) for z in range(8)]
            held[target] = lax.ppermute(held[source], ("z_lo", "z_hi"), steps)
    return [held[offset] for offset in OFFSETS]


def along_x(block, step):
    return lax.ppermute(block, "x", [(i, (i + step) % 4) for i in range(4)])


def to_other_core(block):
    return lax.ppermute(block, "core", [(0, 1), (1, 0)])


def spread_first(whole):
    half = whole.shape[0] // 2
    below, above = along_x(whole, 1), along_x(whole, -1)
    return [whole, below, above, along_x(below[:half], 1), along_x(above[half:], -1)]


def spread_second(first, low, high):
    below_low, above_high = along_x(low, 1), along_x(high, -1)
    below_high, above_low = along_x(high, 1), along_x(low, -1)
    far_low, far_high = along_x(below_low, 1), along_x(above_high, -1)
    mine = [low, high, below_low, below_high, above_low, above_high, far_low, far_high]
    late_low, _ = lax.optimization_barrier((low, far_low))
    late_high, _ = lax.optimization_barrier((high, far_high))
    other = [to_other_core(block) for block in [late_low, late_high] + mine[2:]]
    first_other = []
    for block, gate in zip(first, [low, below_low, above_high, low, high], strict=True):
        late, _ = lax.optimization_barrier((block, gate))
        first_other.append(to_other_core(late))
    return first + first_other, mine + other


def on_device(density, tile_cols, out_cols):
    x, core = lax.axis_index("x"), lax.axis_index("core")
    layer = x * 2 + core
    group = lax.axis_index(("y", "z_lo", "z_hi"))
    own_rows = density.shape[0]
    own = jnp.swapaxes(lax.dynamic_index_in_dim(density, layer, 1, keepdims=False), 1, 2)
    own_a, own_b = own[:, :FIRST], own[:, FIRST:]
    right_b = lax.all_gather(own_b, ("y", "z_hi", "z_lo"), axis=0, tiled=True)
    blocks = tree_gather(own_a)
    square_jobs, cube_jobs = job_lists(tile_cols, out_cols, layer, group, x, core)
    position = jnp.stack([lax.axis_index("y"), lax.axis_index("z_hi") * 2 + lax.axis_index("z_lo")]).astype(jnp.int32)
    left = density.reshape(own_rows * 8, 128, 128)
    square_a, whole_a, right_a = first_square(*square_jobs, position, left, blocks, cube_jobs)
    mine_a = spread_first(whole_a)
    square_b, low_b, high_b = second_square(*square_jobs, left, right_b, ())
    pieces_a, pieces_b = spread_second(mine_a, low_b, high_b)
    purified = cube_part(*cube_jobs, right_a, right_b, square_a, square_b, pieces_a, pieces_b)
    return purified.reshape(own_rows, 1, 4, 128, 128)


def solution(mesh):
    axes = ("y", "z_lo", "z_hi", "x", "core")
    fine = Mesh(mesh.devices.reshape(4, 2, 4, 4, 2), axes)
    rows = ("y", "z_lo", "z_hi")
    return jax.shard_map(
        on_device,
        mesh=fine,
        in_specs=(P(rows, None, None, None), P(), P(rows, None, None)),
        out_specs=P(rows, ("x", "core"), None, None, None),
        check_vma=False,
    )
```

```python
import jax
import jax.numpy as jnp
from jax import lax
from jax.experimental import pallas as pl
from jax.experimental.pallas import tpu as pltpu
from jax.sharding import Mesh
from jax.sharding import PartitionSpec as P

PIECES = 16
GROUP = 4
FIRST = 48
VMEM_LIMIT = 60 * 1024 * 1024
TREE = (
    ((-1, 0), (0, 0), (3, 0)),
    ((0, 1), (0, 0), (0, 1)),
    ((1, 0), (0, 0), (1, 0)),
    ((0, -1), (0, 0), (0, 7)),
    ((-1, 0), (0, 7), (3, 7)),
    ((1, 0), (1, 0), (2, 0)),
    ((0, 1), (1, 0), (1, 1)),
    ((0, -1), (0, 7), (0, 6)),
    ((1, 0), (0, 7), (1, 7)),
    ((0, 1), (0, 1), (0, 2)),
    ((0, -1), (0, 6), (0, 5)),
    ((-1, 0), (0, 1), (3, 1)),
    ((1, 0), (1, 1), (2, 1)),
    ((0, 1), (1, 1), (1, 2)),
    ((0, -1), (2, 0), (2, 7)),
    ((-1, 0), (0, 6), (3, 6)),
    ((0, 1), (0, 2), (0, 3)),
    ((0, -1), (1, 7), (1, 6)),
    ((1, 0), (0, 5), (1, 5)),
    ((-1, 0), (0, 2), (3, 2)),
    ((0, 1), (1, 2), (1, 3)),
    ((0, -1), (0, 5), (0, 4)),
    ((-1, 0), (0, 5), (3, 5)),
    ((1, 0), (1, 2), (2, 2)),
    ((1, 0), (1, 5), (2, 5)),
    ((-1, 0), (3, 6), (2, 6)),
    ((0, -1), (1, 5), (1, 4)),
    ((0, 1), (3, 2), (3, 3)),
    ((0, -1), (3, 5), (3, 4)),
    ((0, 1), (2, 2), (2, 3)),
    ((1, 0), (1, 4), (2, 4)),
)
OFFSETS = tuple((dy, dz) for dy in range(4) for dz in range(8))


def add_products(jobs, count, total, product):
    def body(step, carry):
        first = step * GROUP
        products = [product(first + j) for j in range(GROUP)]
        for j in range(GROUP):
            total[jobs[first + j] & 127] += products[j]
        return carry

    lax.fori_loop(0, (count + GROUP - 1) // GROUP, body, 0)


def square_jobs_run(jobs, count, left, right, total, left_buf, left_sem, right_buf=None, right_sem=None, ready=None):
    def start(j, carry):
        word = jobs[j]
        pltpu.make_async_copy(left.at[(word >> 7) & 127], left_buf.at[j], left_sem).start()
        if right_buf is not None:
            pltpu.make_async_copy(right.at[word >> 14], right_buf.at[j], right_sem).start()
        return carry

    def wait(j, carry):
        pltpu.make_async_copy(left.at[0], left_buf.at[j], left_sem).wait()
        if right_buf is not None:
            pltpu.make_async_copy(right.at[0], right_buf.at[j], right_sem).wait()
        return carry

    def product(j):
        right_tile = right[jobs[j] >> 14] if right_buf is None else right_buf[j]
        return lax.dot_general(right_tile, left_buf[j], (((1,), (1,)), ((), ())), preferred_element_type=jnp.float32)

    lax.fori_loop(0, count, start, 0)
    total[...] = jnp.zeros_like(total)
    if ready is not None:
        ready()
    lax.fori_loop(0, count, wait, 0)
    add_products(jobs, count, total, product)


def write_square(total, square, parts, out_sem):
    copy = pltpu.make_async_copy(total.at[pl.ds(0, square.shape[0])], square, out_sem)
    copy.start()
    first = 0
    for part in parts:
        part[...] = total[first : first + part.shape[0]].astype(jnp.bfloat16)
        first += part.shape[0]
    copy.wait()


def first_square_kernel(jobs, count, position, left, *refs):
    blocks = refs[: len(OFFSETS)]
    square, whole, right, held, left_buf, total, left_sem, block_sem, right_sem, out_sem = refs[-10:]
    size = blocks[0].shape[0]
    for (dy, dz), block in zip(OFFSETS, blocks, strict=True):
        from_y = (position[0] + (4 - dy)) & 3
        from_z = (position[1] + (8 - dz)) & 7
        pltpu.make_async_copy(block, held.at[pl.ds((from_y * 8 + from_z) * size, size)], block_sem).start()

    def ready():
        pltpu.make_async_copy(held, held, block_sem).wait()
        pltpu.make_async_copy(held, right, right_sem).start()

    square_jobs_run(jobs, count[0], left, held, total, left_buf, left_sem, ready=ready)
    write_square(total, square, [whole], out_sem)
    pltpu.make_async_copy(held, right, right_sem).wait()


def second_square_kernel(jobs, count, left, right, *refs):
    square, low, high, left_buf, right_buf, total, left_sem, right_sem, out_sem = refs[-9:]
    square_jobs_run(jobs, count[0], left, right, total, left_buf, left_sem, right_buf, right_sem)
    write_square(total, square, [low, high], out_sem)


SMEM = pl.BlockSpec(memory_space=pltpu.SMEM)
VMEM = pl.BlockSpec(memory_space=pltpu.VMEM)
HBM = pl.BlockSpec(memory_space=pltpu.HBM)


def square_outs(part, cuts):
    low = jax.ShapeDtypeStruct((64 // cuts, part, 128), jnp.bfloat16)
    return (jax.ShapeDtypeStruct((64, part, 128), jnp.float32),) + (low,) * cuts


def first_square(jobs, count, position, left, blocks, after):
    size, part = blocks[0].shape[:2]
    return pl.pallas_call(
        first_square_kernel,
        out_shape=square_outs(part, 1) + (jax.ShapeDtypeStruct((len(blocks) * size, part, 128), jnp.bfloat16),),
        in_specs=[SMEM, SMEM, SMEM] + [HBM] * (1 + len(blocks) + len(after)),
        out_specs=(HBM, VMEM, HBM),
        scratch_shapes=[
            pltpu.VMEM((len(blocks) * size, part, 128), jnp.bfloat16),
            pltpu.VMEM((jobs.shape[0], 128, 128), jnp.bfloat16),
            pltpu.VMEM((65, part, 128), jnp.float32),
            pltpu.SemaphoreType.DMA,
            pltpu.SemaphoreType.DMA,
            pltpu.SemaphoreType.DMA,
            pltpu.SemaphoreType.DMA,
        ],
        compiler_params=pltpu.CompilerParams(vmem_limit_bytes=VMEM_LIMIT),
        name="first_square",
    )(jobs, count, position, left, *blocks, *after)


def second_square(jobs, count, left, right, after):
    part = right.shape[1]
    return pl.pallas_call(
        second_square_kernel,
        out_shape=square_outs(part, 2),
        in_specs=[SMEM, SMEM, HBM, HBM] + [HBM] * len(after),
        out_specs=(HBM, VMEM, VMEM),
        scratch_shapes=[
            pltpu.VMEM((jobs.shape[0], 128, 128), jnp.bfloat16),
            pltpu.VMEM((jobs.shape[0], part, 128), jnp.bfloat16),
            pltpu.VMEM((65, part, 128), jnp.float32),
            pltpu.SemaphoreType.DMA,
            pltpu.SemaphoreType.DMA,
            pltpu.SemaphoreType.DMA,
        ],
        compiler_params=pltpu.CompilerParams(vmem_limit_bytes=VMEM_LIMIT),
        name="second_square",
    )(jobs, count, left, right, *after)


def cube_kernel(*refs):
    jobs, bounds, right_a, right_b, square_a, square_b = refs[:6]
    pieces_a, pieces_b = refs[6:16], refs[16 : 16 + PIECES]
    out, right_buf, left_buf, total, square, right_sem, left_sem, square_sem = refs[16 + PIECES :]
    first_part = square_a.shape[1]
    rest = 128 - first_part
    count = bounds[PIECES]
    for p in range(PIECES):
        kind, half = p % 8 // 2, p % 2
        whole = kind < 3
        piece_a = pieces_a[p // 8 * 5 + (kind if whole else 3 + half)]
        shift = 32 * half if whole else 0

        def start(j, carry, p=p, piece_a=piece_a, shift=shift):
            word = jobs[j]
            place = word >> 17
            at = (word >> 7) & 63
            top, bottom = pl.ds(0, first_part), pl.ds(first_part, rest)
            pltpu.make_async_copy(piece_a.at[at + shift], left_buf.at[j, top], left_sem).start()
            pltpu.make_async_copy(pieces_b[p].at[at], left_buf.at[j, bottom], left_sem).start()
            pltpu.make_async_copy(right_a.at[place], right_buf.at[j, top], right_sem).start()
            pltpu.make_async_copy(right_b.at[place], right_buf.at[j, bottom], right_sem).start()
            return carry

        lax.fori_loop(bounds[p], bounds[p + 1], start, 0)
    pltpu.make_async_copy(square_a, square.at[:, pl.ds(0, first_part)], square_sem).start()
    pltpu.make_async_copy(square_b, square.at[:, pl.ds(first_part, rest)], square_sem).start()
    total[...] = jnp.zeros_like(total)

    def wait(j, carry):
        pltpu.make_async_copy(left_buf.at[j], left_buf.at[j], left_sem).wait()
        pltpu.make_async_copy(right_buf.at[j], right_buf.at[j], right_sem).wait()
        return carry

    def product(j):
        return jnp.dot(right_buf[j], left_buf[j], preferred_element_type=jnp.float32)

    lax.fori_loop(0, count, wait, 0)
    add_products(jobs, count, total, product)
    pltpu.make_async_copy(square, square, square_sem).wait()

    def finish(step, carry):
        for j in range(GROUP):
            o = step * GROUP + j
            out[o] = (3.0 * square[o] - 2.0 * total[o]).T.astype(jnp.bfloat16)
        return carry

    lax.fori_loop(0, out.shape[0] // GROUP, finish, 0)


def cube_part(jobs, bounds, right_a, right_b, square_a, square_b, pieces_a, pieces_b):
    return pl.pallas_call(
        cube_kernel,
        out_shape=jax.ShapeDtypeStruct((64, 128, 128), jnp.bfloat16),
        in_specs=[SMEM, SMEM] + [HBM] * (14 + PIECES),
        out_specs=VMEM,
        scratch_shapes=[
            pltpu.VMEM((jobs.shape[0], 128, 128), jnp.bfloat16),
            pltpu.VMEM((jobs.shape[0], 128, 128), jnp.bfloat16),
            pltpu.VMEM((65, 128, 128), jnp.float32),
            pltpu.VMEM((64, 128, 128), jnp.float32),
            pltpu.SemaphoreType.DMA,
            pltpu.SemaphoreType.DMA,
            pltpu.SemaphoreType.DMA,
        ],
        compiler_params=pltpu.CompilerParams(vmem_limit_bytes=VMEM_LIMIT),
        name="cube_part",
    )(jobs, bounds, right_a, right_b, square_a, square_b, *pieces_a, *pieces_b)


def packed_jobs(matched, payload, kind):
    total = matched.shape[0]
    ids = jnp.arange(total, dtype=jnp.int32)
    order = kind * total + ids
    hits = matched.astype(jnp.int32)
    rank = jnp.sum(jnp.where(order[None, :] < order[:, None], hits[None, :], 0), axis=1)
    chosen = (rank[None, :] == ids[:, None]) & matched[None, :]
    words = jnp.sum(jnp.where(chosen, payload[None, :], 0), axis=1)
    count = jnp.sum(hits)
    return jnp.where(ids < count, words, 64).astype(jnp.int32), count[None]


def place_of(k):
    group, within = k // 16, k % 16
    y, z_lo, z_hi = group // 8, (group // 4) % 2, group % 4
    return ((y * 4 + z_hi) * 2 + z_lo) * 16 + within


def target_slots(tile_cols, out_cols, layer, index):
    colset = lax.dynamic_index_in_dim(tile_cols, layer, 1, keepdims=False)
    wanted = lax.dynamic_index_in_dim(out_cols, layer, 1, keepdims=False)
    every = jnp.arange(tile_cols.shape[0], dtype=jnp.int32)
    reached = jnp.sum(jnp.where(index[..., None] == every, colset, 0), axis=-1)
    same = reached[:, :, None] == wanted[:, None, :]
    slot = jnp.sum(jnp.where(same, jnp.arange(4, dtype=jnp.int32), 0), axis=-1)
    rows = jnp.arange(index.shape[0], dtype=jnp.int32)[:, None]
    return jnp.any(same, axis=-1), rows * 4 + slot


def square_list(tile_cols, out_cols, layer, group):
    own_rows = out_cols.shape[0]
    own_cols = lax.dynamic_slice_in_dim(tile_cols, group * own_rows, own_rows, 0)
    matched, target = target_slots(tile_cols, out_cols, layer, own_cols)
    source = jnp.arange(own_rows * 8, dtype=jnp.int32).reshape(own_rows, 8)
    words = (place_of(own_cols) << 14) | (source << 7) | target
    return packed_jobs(matched.reshape(-1), words.reshape(-1), 0)


def cube_list(tile_cols, out_cols, layer, x, core):
    own_rows = out_cols.shape[0]
    through = out_cols.reshape(own_rows, 32)
    matched, target = target_slots(tile_cols, out_cols, layer, through)
    rows = jnp.arange(own_rows, dtype=jnp.int32)[:, None]
    m = jnp.arange(32, dtype=jnp.int32)[None, :]
    u, t = m // 4, m % 4
    distance = (u // 2 - x) % 4
    half = rows // (own_rows // 2)
    piece = jnp.where(distance == 3, 2, jnp.where(distance == 1, 4, jnp.where(distance == 2, 6, 0))) + half
    piece = piece + jnp.where(u % 2 == core, 0, PIECES // 2)
    at = rows % (own_rows // 2) * 4 + t
    words = (place_of(through) << 17) | (piece << 13) | (at << 7) | target
    matched, piece = matched.reshape(-1), piece.reshape(-1)
    jobs, _ = packed_jobs(matched, words.reshape(-1), piece)
    below = piece[None, :] < jnp.arange(PIECES + 1, dtype=jnp.int32)[:, None]
    bounds = jnp.sum((below & matched[None, :]).astype(jnp.int32), axis=1)
    return jobs, bounds


def tree_gather(own):
    ring = [(z % 2) * 4 + z // 2 for z in range(8)]
    held = {(0, 0): own}
    for (dy, dz), source, target in TREE:
        if dy:
            held[target] = lax.ppermute(held[source], "y", [(i, (i + dy) % 4) for i in range(4)])
        else:
            steps = [(ring[z], ring[(z + dz) % 8]) for z in range(8)]
            held[target] = lax.ppermute(held[source], ("z_lo", "z_hi"), steps)
    return [held[offset] for offset in OFFSETS]


def along_x(block, step):
    return lax.ppermute(block, "x", [(i, (i + step) % 4) for i in range(4)])


def to_other_core(block):
    return lax.ppermute(block, "core", [(0, 1), (1, 0)])


def spread_first(whole):
    half = whole.shape[0] // 2
    below, above = along_x(whole, 1), along_x(whole, -1)
    return [whole, below, above, along_x(below[:half], 1), along_x(above[half:], -1)]


def spread_second(first, low, high):
    below_low, above_high = along_x(low, 1), along_x(high, -1)
    below_high, above_low = along_x(high, 1), along_x(low, -1)
    far_low, far_high = along_x(below_low, 1), along_x(above_high, -1)
    mine = [low, high, below_low, below_high, above_low, above_high, far_low, far_high]
    late_low, _ = lax.optimization_barrier((low, far_low))
    late_high, _ = lax.optimization_barrier((high, far_high))
    other = [to_other_core(block) for block in [late_low, late_high] + mine[2:]]
    first_other = []
    for block, gate in zip(first, [low, below_low, above_high, low, high], strict=True):
        late, _ = lax.optimization_barrier((block, gate))
        first_other.append(to_other_core(late))
    return first + first_other, mine + other


def on_device(density, tile_cols, out_cols):
    x, core = lax.axis_index("x"), lax.axis_index("core")
    layer = x * 2 + core
    group = lax.axis_index(("y", "z_lo", "z_hi"))
    own_rows = density.shape[0]
    own = jnp.swapaxes(lax.dynamic_index_in_dim(density, layer, 1, keepdims=False), 1, 2)
    own_a, own_b = own[:, :FIRST], own[:, FIRST:]
    right_b = lax.all_gather(own_b, ("y", "z_hi", "z_lo"), axis=0, tiled=True)
    blocks = tree_gather(own_a)
    square_jobs = square_list(tile_cols, out_cols, layer, group)
    position = jnp.stack([lax.axis_index("y"), lax.axis_index("z_hi") * 2 + lax.axis_index("z_lo")]).astype(jnp.int32)
    left = density.reshape(own_rows * 8, 128, 128)
    square_a, whole_a, right_a = first_square(*square_jobs, position, left, blocks, ())
    mine_a = spread_first(whole_a)
    late_cols, late_out, _ = lax.optimization_barrier((tile_cols, out_cols, whole_a[0, 0, :1]))
    cube_jobs = cube_list(late_cols, late_out, layer, x, core)
    square_b, low_b, high_b = second_square(*square_jobs, left, right_b, cube_jobs)
    pieces_a, pieces_b = spread_second(mine_a, low_b, high_b)
    purified = cube_part(*cube_jobs, right_a, right_b, square_a, square_b, pieces_a, pieces_b)
    return purified.reshape(own_rows, 1, 4, 128, 128)


def solution(mesh):
    axes = ("y", "z_lo", "z_hi", "x", "core")
    fine = Mesh(mesh.devices.reshape(4, 2, 4, 4, 2), axes)
    rows = ("y", "z_lo", "z_hi")
    return jax.shard_map(
        on_device,
        mesh=fine,
        in_specs=(P(rows, None, None, None), P(), P(rows, None, None)),
        out_specs=P(rows, ("x", "core"), None, None, None),
        check_vma=False,
    )
```
